32 devices in a mesh: member: 2 (over x), tile: 8 (over z, core), grp: 2 (over y).
Axes of the slice: x: 2, y: 2, z: 4, core: 2. Of those that a mesh axis runs over, the one named last changes fastest.
Arguments:
- latent: bfloat16 [4096, 768], P('tile'), may hold values from -6 to 6
- noise: bfloat16 [4, 4096, 768], P(('member', 'grp'), 'tile'), may hold values from -6 to 6
- area: float32 [4096], P('tile'), may hold values from 0.3 to 9, as said below
- target: float32 [13], replicated, may hold values from -1 to 1
- truth: float32 [80, 4096], P(('member', 'grp'), 'tile'), may hold values from -6 to 6
- neighbours: int32 [4096, 4], P('tile'), may hold values from 0 to 4095, as said below
- w_up: bfloat16 [2, 768, 1536], P(None, 'tile'), may hold values from -0.21875 to 0.21875
- w_down: bfloat16 [2, 1536, 768], P(None, 'tile'), may hold values from -0.15625 to 0.15625
- w_out: bfloat16 [768, 80], P('tile'), may hold values from -0.21875 to 0.21875
Outputs:
- score: float32 [80, 4096], P(('member', 'grp'), 'tile')
- grad_up: float32 [2, 768, 1536], P(None, 'tile')
- grad_down: float32 [2, 1536, 768], P(None, 'tile')
- grad_out: float32 [768, 80], P('tile')
The draws below stay inside these ranges and needn't reach their ends.
Inputs may be any that keep to these rules, and one draw needn't show every extreme that they name: neighbours[i, k] lies within 32 steps of i in the cyclic order of nodes; for every node one neighbour is exactly 32 steps ahead and another exactly 32 steps behind. `area`: positive.
All inputs are finite; a program needn't handle non-finite values.
Results may differ from the reference program's by a relative error of at most 0.0045.
Values may be sent and summed in bfloat16 or wider, within the bound.
A program may use at most 128 MiB of HBM per device.

```python
import math
import jax
import jax.numpy as jnp
from jax import lax

D = 768
FF = 1536
C_OUT = 80
TEMP = 13
NEIGH = 4
HALO = 32
LAYERS = 2
MEMBERS = 4
NODES = 4096


def draw_area(key, part):
    key = jax.random.fold_in(key, 11)
    position = jnp.arange(NODES, dtype=jnp.float32) / (NODES - 1)
    local_weight = jnp.exp(jax.random.uniform(key, (NODES,), jnp.float32, math.log(0.3), math.log(3.0)))
    return (1.0 + 2.0 * position) * local_weight


def draw_neighbours(key, part):
    key = jax.random.fold_in(key, 23)
    side_key, other_key = jax.random.split(key)
    node_index = jnp.arange(NODES, dtype=jnp.int32)
    side_sign = 2 * jax.random.randint(side_key, (NODES,), 0, 2, dtype=jnp.int32) - 1
    first_column = (node_index + HALO * side_sign) % NODES
    second_column = (node_index - HALO * side_sign) % NODES
    steps_drawn = jax.random.randint(other_key, (NODES, NEIGH - 2), -HALO, HALO + 1, dtype=jnp.int32)
    other_columns = (node_index[:, None] + steps_drawn) % NODES
    return jnp.concatenate([first_column[:, None], second_column[:, None], other_columns], axis=1)


def block_scale(rng, extent, shards, smallest, largest):
    gain, own = 1.0, jax.random.fold_in(rng, 6)
    for axis_at, parts in shards:
        draws = jnp.exp(jax.random.uniform(jax.random.fold_in(own, axis_at), (parts,), jnp.float32, smallest / len(shards), largest / len(shards)))
        gain = gain * jnp.repeat(draws, extent[axis_at] // parts).reshape([-1 if axis == axis_at else 1 for axis in range(len(extent))])
    return gain


def bell_draw(own_key, extent, deviation, most, shards=(), kind=jnp.bfloat16):
    drawn = deviation * jax.random.normal(own_key, extent, jnp.float32)
    if shards:
        drawn = drawn * block_scale(own_key, extent, shards, -0.22, 0.18)
    return jnp.clip(drawn, -most, most).astype(kind)


def setup_inputs(seed: int = 0) -> dict:
    streams_of = jax.random.split(jax.random.key(seed), 10)
    latent = bell_draw(streams_of[0], (NODES, D), 1.0, 6.0, ((0, 8),))
    noise = bell_draw(streams_of[1], (MEMBERS, NODES, D), 1.0, 6.0, ((0, 4), (1, 8)))
    area = draw_area(jax.random.fold_in(streams_of[9], 71), 0)
    target = jnp.clip(jax.random.uniform(streams_of[3], (TEMP,), jnp.float32, -1.0, 1.0), -1.0, 1.0)
    truth = bell_draw(streams_of[4], (C_OUT, NODES), 1.0, 6.0, ((0, 4), (1, 8)), jnp.float32)
    neighbours = draw_neighbours(jax.random.fold_in(streams_of[9], 71), 0)
    w_up = bell_draw(streams_of[6], (LAYERS, D, FF), D ** -0.5, 0.21875, ((1, 8),))
    w_down = bell_draw(streams_of[7], (LAYERS, FF, D), FF ** -0.5, 0.15625, ((1, 8),))
    w_out = bell_draw(streams_of[8], (D, C_OUT), D ** -0.5, 0.21875, ((0, 8),))
    return dict(latent=latent, noise=noise, area=area, target=target, truth=truth, neighbours=neighbours, w_up=w_up, w_down=w_down, w_out=w_out)


EPSILON = 1e-06
SOFTNESS = 0.25
SOFT_ROOT = 0.5

def normalize(values):
    return values * lax.rsqrt(lax.optimization_barrier(jnp.mean(values * values, axis=-1, keepdims=True)) + EPSILON)

def distance_kernel(offset):
    return jnp.sqrt(offset * offset + SOFTNESS) - SOFT_ROOT

def kernel_slope(offset):
    return offset / jnp.sqrt(offset * offset + SOFTNESS)

def blend_rows(normed, neighbours):
    summed = normed[neighbours[:, 0]].astype(jnp.float32)
    for column in range(1, NEIGH):
        summed = summed + normed[neighbours[:, column]].astype(jnp.float32)
    return (normed.astype(jnp.float32) + summed / NEIGH).astype(jnp.bfloat16)

def unblend_rows(grad_blend, neighbours):
    result = grad_blend
    portion = grad_blend / NEIGH
    for column in range(NEIGH):
        result = result.at[neighbours[:, column]].add(portion)
    return result

def forward_member(initial, neighbours, w_up, w_down, w_out):
    hidden_state = initial
    stored = []
    for layer_index in range(LAYERS):
        blended = blend_rows(normalize(hidden_state).astype(jnp.bfloat16), neighbours)
        preact = jnp.dot(blended, w_up[layer_index], preferred_element_type=jnp.float32)
        hidden = jax.nn.gelu(preact).astype(jnp.bfloat16)
        stored.append((hidden_state, blended, preact, hidden))
        hidden_state = hidden_state + jnp.dot(hidden, w_down[layer_index], preferred_element_type=jnp.float32)
    final_normed = normalize(hidden_state).astype(jnp.bfloat16)
    predicted = jnp.dot(final_normed, w_out, preferred_element_type=jnp.float32)
    return (predicted, hidden_state, final_normed, stored)

def reference(latent, noise, area, target, truth, neighbours, w_up, w_down, w_out):
    initial_base = latent.astype(jnp.float32)
    area_total = jnp.sum(area)

    def run_member(member_noise):
        predicted = forward_member(initial_base + member_noise.astype(jnp.float32), neighbours, w_up, w_down, w_out)[0]
        weighted = jnp.dot(area, predicted[:, :TEMP], precision=lax.Precision.HIGHEST)
        nudged = predicted.at[:, :TEMP].add(target - weighted / area_total)
        return nudged.T
    ensemble = lax.map(run_member, noise)
    members = noise.shape[0]
    against = ensemble - truth[None]
    skill_term = lax.optimization_barrier(jnp.mean(distance_kernel(against), axis=0))
    spread = jnp.zeros_like(truth)
    slope_sum = jnp.zeros_like(ensemble)
    for other in range(members):
        pair_gap = ensemble - ensemble[other][None]
        spread = spread + lax.optimization_barrier(jnp.sum(distance_kernel(pair_gap), axis=0))
        slope_sum = slope_sum + kernel_slope(pair_gap)
    score_field = skill_term - spread / (2 * members * (members - 1))
    cotangent = kernel_slope(against) / members - slope_sum / (members * (members - 1))
    column_sums = lax.optimization_barrier(jnp.sum(cotangent[:, :TEMP], axis=2))
    cotangent = cotangent.at[:, :TEMP].add(-(area[None, None, :] * (column_sums[:, :, None] / area_total)))

    def member_grads(running, member_item):
        member_noise, member_cot = member_item
        predicted, final_state, final_normed, stored = forward_member(initial_base + member_noise.astype(jnp.float32), neighbours, w_up, w_down, w_out)
        upstream = member_cot.T.astype(jnp.bfloat16)
        grad_output = jnp.dot(final_normed.T, upstream, preferred_element_type=jnp.float32)
        grad_final = jnp.dot(upstream, w_out.T, preferred_element_type=jnp.float32)
        grad_state = jax.vjp(normalize, final_state)[1](grad_final)[0]
        ups_list = []
        downs_list = []
        for layer_index in reversed(range(LAYERS)):
            hidden_state, blended, preact, hidden = stored[layer_index]
            flowing = grad_state.astype(jnp.bfloat16)
            downs_list.insert(0, jnp.dot(hidden.T, flowing, preferred_element_type=jnp.float32))
            grad_hidden = jnp.dot(flowing, w_down[layer_index].T, preferred_element_type=jnp.float32)
            grad_preact = jax.vjp(jax.nn.gelu, preact)[1](grad_hidden)[0].astype(jnp.bfloat16)
            ups_list.insert(0, jnp.dot(blended.T, grad_preact, preferred_element_type=jnp.float32))
            grad_blend = jnp.dot(grad_preact, w_up[layer_index].T, preferred_element_type=jnp.float32)
            grad_normed = unblend_rows(grad_blend, neighbours)
            grad_state = grad_state + jax.vjp(normalize, hidden_state)[1](grad_normed)[0]
        sum_up, sum_down, sum_out = running
        return ((sum_up + jnp.stack(ups_list), sum_down + jnp.stack(downs_list), sum_out + grad_output), None)
    start_sums = (jnp.zeros(w_up.shape, jnp.float32), jnp.zeros(w_down.shape, jnp.float32), jnp.zeros(w_out.shape, jnp.float32))
    totals, _ = lax.scan(member_grads, start_sums, (noise, cotangent))
    return (score_field, totals[0], totals[1], totals[2])
```

```python
import jax
import jax.numpy as jnp
from jax import lax
from jax.sharding import PartitionSpec as P

TEMP = 13
NEIGH = 4
HALO = 32
LAYERS = 2


EPSILON = 1e-06
SOFTNESS = 0.25
SOFT_ROOT = 0.5
SHARE = jnp.bfloat16


def padded(cells, sides, width):
    for axis, dim in sides:
        count = lax.axis_size(axis)
        head = lax.slice_in_dim(cells, 0, width, axis=dim)
        tail = lax.slice_in_dim(cells, cells.shape[dim] - width, cells.shape[dim], axis=dim)
        cells = jnp.concatenate(
            [
                lax.ppermute(tail, axis, [(i, (i + 1) % count) for i in range(count)]),
                cells,
                lax.ppermute(head, axis, [((i + 1) % count, i) for i in range(count)]),
            ],
            axis=dim,
        )
    return cells


def passed_along(block, axis, distance):
    devices = range(lax.axis_size(axis))
    route = [((i - distance) % len(devices), i) for i in devices]
    return lax.ppermute(block, axis, route)


def normalize(values):
    return values * lax.rsqrt(jnp.mean(values * values, axis=-1, keepdims=True) + EPSILON)


def distance_kernel(offset):
    return jnp.sqrt(offset * offset + SOFTNESS) - SOFT_ROOT


def kernel_slope(offset):
    return offset / jnp.sqrt(offset * offset + SOFTNESS)


def paired():
    return lax.axis_size("member") == 2 and lax.axis_size("grp") == 2


def swapped(block, axis):
    return lax.ppermute(block, axis, [(0, 1), (1, 0)])


def core_swapped(block):
    return lax.ppermute(block, "tile", [(i, i ^ 1) for i in range(lax.axis_size("tile"))])


def shifted(block, distance):
    count = lax.axis_size("tile")
    chips = count // 2
    route = [(i, (i // 2 + distance) % chips * 2 + i % 2) for i in range(count)]
    return lax.ppermute(block, "tile", route)


def tile_sum(values):
    count = lax.axis_size("tile")
    if count & (count - 1):
        return lax.psum(values, "tile")
    step = 1
    while step < count:
        values = values + lax.ppermute(values, "tile", [(i, i ^ step) for i in range(count)])
        step *= 2
    return values


def pick(block, index, dim):
    return lax.dynamic_index_in_dim(block, index, dim, keepdims=False)


def half(block, index, dim):
    size = block.shape[dim] // 2
    return lax.dynamic_slice_in_dim(block, index * size, size, axis=dim)


def halved(block, index, dim, axis):
    got = swapped(half(block, 1 - index, dim).astype(jnp.bfloat16), axis)
    return half(block, index, dim) + got.astype(jnp.float32)


def blend_matrix(local_index, nodes_dev):
    column = jnp.arange(nodes_dev + 2 * HALO, dtype=jnp.int32)[None, :]
    row = jnp.arange(nodes_dev, dtype=jnp.int32)[:, None]
    total = (column == row + HALO).astype(jnp.float32)
    for k in range(NEIGH):
        total = total + jnp.where(column == local_index[:, k : k + 1], 1.0 / NEIGH, 0.0)
    return total.astype(jnp.bfloat16)


def blend_local(normed, matrix):
    extended = padded(normed, (("tile", 0),), HALO)
    return jnp.dot(matrix, extended, preferred_element_type=jnp.float32).astype(jnp.bfloat16)


def unblend_local(grad_blend, matrix):
    nodes_dev = grad_blend.shape[0]
    coarse = lax.reduce_precision(grad_blend, 8, 7)
    fine = (grad_blend - coarse).astype(jnp.bfloat16)
    extended = jnp.dot(
        matrix.T, coarse.astype(jnp.bfloat16), preferred_element_type=jnp.float32
    ) + jnp.dot(matrix.T, fine, preferred_element_type=jnp.float32)
    from_next = passed_along(extended[:HALO], "tile", -1)
    from_prev = passed_along(extended[nodes_dev + HALO :], "tile", 1)
    result = extended[HALO : nodes_dev + HALO]
    result = result.at[nodes_dev - HALO :].add(from_next)
    return result.at[:HALO].add(from_prev)


def core_reduced(left, right):
    count = lax.axis_size("tile")
    core = lax.axis_index("tile") % 2
    grouped = left.reshape(left.shape[0], count // 2, 2, -1)
    rows = left.shape[1] // 2

    def product(which):
        chosen = pick(grouped, which, 2).reshape(left.shape[0], rows)
        return jnp.dot(chosen.T, right, preferred_element_type=jnp.float32)

    got = core_swapped(product(1 - core).astype(jnp.bfloat16))
    total = product(core) + got.astype(jnp.float32)
    return total.reshape(count // 2, -1, right.shape[1])


def reduced_widely(down, up):
    chips = lax.axis_size("tile") // 2
    chip = lax.axis_index("tile") // 2
    totals = []
    for parts in (down, up):
        total = pick(parts, chip, 0)
        for k in range(1, chips):
            sent = pick(parts, (chip + k) % chips, 0).astype(jnp.bfloat16)
            total = total + shifted(sent, k).astype(jnp.float32)
        totals.append(lax.psum(total, ("member", "grp")))
    return tuple(totals)


def reduced(down, up):
    if not paired():
        return reduced_widely(down, up)
    chips = lax.axis_size("tile") // 2
    chip = lax.axis_index("tile") // 2
    x = lax.axis_index("member")
    y = lax.axis_index("grp")
    rows = down.shape[1] // 2
    width = down.shape[2]
    first = jnp.stack([down[:, :rows], up[:, :, :width]])
    second = jnp.stack([down[:, rows:], up[:, :, width:]])
    first = halved(first, x, 2, "member")
    second = halved(second, y, 2, "grp")
    first = halved(first, y, 3, "grp")
    second = halved(second, x, 3, "member")
    both = jnp.stack([first, second])
    total = pick(both, chip, 2)
    for k in range(1, chips):
        sent = pick(both, (chip + k) % chips, 2).astype(jnp.bfloat16)
        total = total + shifted(sent, k).astype(jnp.float32)
    own = total.astype(SHARE)
    grid = [(m, g) for m in range(2) for g in range(2)]

    def from_corner(dm, dg):
        if not (dm or dg):
            return own
        route = [(2 * m + g, 2 * (m ^ dm) + (g ^ dg)) for m, g in grid]
        return lax.ppermute(own, ("member", "grp"), route)

    corners = [from_corner(m, g) for m, g in grid]
    west = [jnp.where(x == 0, corners[g], corners[2 + g]) for g in range(2)]
    east = [jnp.where(x == 0, corners[2 + g], corners[g]) for g in range(2)]

    def ordered(pair):
        return (jnp.where(y == 0, pair[0], pair[1]), jnp.where(y == 0, pair[1], pair[0]))

    (a00, a01), (a10, a11) = ordered(west), ordered(east)

    def tiled(p, q, r, s, part):
        top = jnp.concatenate([p[part], q[part]], axis=2)
        low = jnp.concatenate([r[part], s[part]], axis=2)
        return jnp.concatenate([top, low], axis=1).astype(jnp.float32)

    first = tiled(a00, a01, a10, a11, 0)
    second = tiled(a00, a10, a01, a11, 1)
    return (
        jnp.concatenate([first[0], second[0]], axis=0),
        jnp.concatenate([first[1], second[1]], axis=1),
    )


def reduced_out(left, right):
    chips = lax.axis_size("tile") // 2
    chip = lax.axis_index("tile") // 2
    core = lax.axis_index("tile") % 2
    whole = jnp.dot(left.T, right, preferred_element_type=jnp.float32)
    whole = whole.reshape(chips, 2, -1, right.shape[1])
    total = pick(whole, core, 1) + core_swapped(pick(whole, 1 - core, 1))
    mine = pick(total, chip, 0)
    for k in range(1, chips):
        mine = mine + shifted(pick(total, (chip + k) % chips, 0), k)
    if not paired():
        return lax.psum(mine, ("member", "grp"))
    mine = mine + swapped(mine, "member")
    return mine + swapped(mine, "grp")


def gathered_out(block):
    chips = lax.axis_size("tile") // 2
    chip = lax.axis_index("tile") // 2
    core = lax.axis_index("tile") % 2
    other = core_swapped(block)
    pair = jnp.concatenate(
        [jnp.where(core == 0, block, other), jnp.where(core == 0, other, block)], axis=0
    )
    parts = jnp.stack([pair] + [shifted(pair, k) for k in range(1, chips)])
    order = (chip - jnp.arange(chips)) % chips
    return jnp.concatenate([pick(parts, order[z], 0) for z in range(chips)], axis=0)


def shards(latent, noise, area, target, truth, neighbours, w_up, w_down, w_out):
    nodes_dev = latent.shape[0]
    total_nodes = nodes_dev * lax.axis_size("tile")
    row_ids = jnp.arange(nodes_dev, dtype=jnp.int32)
    global_rows = lax.axis_index("tile") * nodes_dev + row_ids
    local_index = (neighbours - global_rows[:, None] + HALO) % total_nodes + row_ids[:, None]
    full_up = [lax.all_gather(w_up[l], "tile", axis=0, tiled=True) for l in range(LAYERS)]
    full_down = [lax.all_gather(w_down[l], "tile", axis=0, tiled=True) for l in range(LAYERS)]
    full_out = gathered_out(w_out)
    matrix = blend_matrix(local_index, nodes_dev)
    hidden_state = latent.astype(jnp.float32) + noise[0].astype(jnp.float32)
    stored = []
    for layer_index in range(LAYERS):
        blended = blend_local(normalize(hidden_state).astype(jnp.bfloat16), matrix)
        preact = jnp.dot(blended, full_up[layer_index], preferred_element_type=jnp.float32)
        hidden = jax.nn.gelu(preact).astype(jnp.bfloat16)
        stored.append((hidden_state, blended, preact, hidden))
        hidden_state = hidden_state + jnp.dot(
            hidden, full_down[layer_index], preferred_element_type=jnp.float32
        )
    final_state = hidden_state
    final_normed = normalize(final_state).astype(jnp.bfloat16)
    predicted = jnp.dot(final_normed, full_out, preferred_element_type=jnp.float32)
    channels = predicted.shape[1]
    block_size = channels // lax.axis_size(("member", "grp"))
    first_channel = lax.axis_index(("member", "grp")) * block_size
    is_temp = first_channel + jnp.arange(block_size, dtype=jnp.int32) < TEMP
    local_sums = jnp.concatenate(
        [
            jnp.dot(area, predicted[:, :TEMP], precision=lax.Precision.HIGHEST),
            jnp.sum(area)[None],
        ]
    )
    sums = tile_sum(local_sums)
    weighted, area_total = sums[:TEMP], sums[TEMP]
    nudged = predicted.at[:, :TEMP].add(target - weighted / area_total)
    ensemble = lax.all_to_all(
        nudged.T[None], ("member", "grp"), split_axis=1, concat_axis=0, tiled=True
    )
    members = ensemble.shape[0]
    against = ensemble - truth[None]
    skill_term = jnp.mean(distance_kernel(against), axis=0)
    pair_gaps = ensemble[:, None] - ensemble[None, :]
    spread = jnp.sum(distance_kernel(pair_gaps), axis=(0, 1))
    slope_sum = jnp.sum(kernel_slope(pair_gaps), axis=1)
    score_field = skill_term - spread / (2 * members * (members - 1))
    cotangent = kernel_slope(against) / members - slope_sum / (members * (members - 1))
    column_sums = tile_sum(jnp.sum(cotangent, axis=2))
    correction = jnp.where(is_temp[None, :], column_sums, 0.0)
    cotangent = cotangent - area[None, None, :] * (correction[:, :, None] / area_total)
    returned = lax.all_to_all(
        cotangent, ("member", "grp"), split_axis=0, concat_axis=1, tiled=True
    )[0]
    upstream = returned.T.astype(jnp.bfloat16)
    sum_out = reduced_out(final_normed, upstream)
    grad_final = jnp.dot(upstream, full_out.T, preferred_element_type=jnp.float32)
    grad_state = jax.vjp(normalize, final_state)[1](grad_final)[0]
    ups_list = []
    downs_list = []
    for layer_index in reversed(range(LAYERS)):
        hidden_state, blended, preact, hidden = stored[layer_index]
        flowing = grad_state.astype(jnp.bfloat16)
        down = core_reduced(hidden, flowing)
        grad_hidden = jnp.dot(flowing, full_down[layer_index].T, preferred_element_type=jnp.float32)
        grad_preact = jax.vjp(jax.nn.gelu, preact)[1](grad_hidden)[0].astype(jnp.bfloat16)
        sum_down, sum_up = reduced(down, core_reduced(blended, grad_preact))
        downs_list.insert(0, sum_down)
        ups_list.insert(0, sum_up)
        if layer_index == 0:
            break
        grad_blend = jnp.dot(
            grad_preact, full_up[layer_index].T, preferred_element_type=jnp.float32
        )
        grad_normed = unblend_local(grad_blend, matrix)
        grad_state = grad_state + jax.vjp(normalize, hidden_state)[1](grad_normed)[0]
    return (score_field, jnp.stack(ups_list), jnp.stack(downs_list), sum_out)


def solution(mesh):
    return jax.shard_map(
        shards,
        mesh=mesh,
        in_specs=(
            P("tile", None),
            P(("member", "grp"), "tile", None),
            P("tile"),
            P(),
            P(("member", "grp"), "tile"),
            P("tile", None),
            P(None, "tile", None),
            P(None, "tile", None),
            P("tile", None),
        ),
        out_specs=(
            P(("member", "grp"), "tile"),
            P(None, "tile", None),
            P(None, "tile", None),
            P("tile", None),
        ),
        check_vma=False,
    )
```

```python
import jax
import jax.numpy as jnp
from jax import lax
from jax.sharding import PartitionSpec as P

TEMP = 13
NEIGH = 4
HALO = 32
LAYERS = 2


EPSILON = 1e-06
SOFTNESS = 0.25
SOFT_ROOT = 0.5
SHARE = jnp.bfloat16


def padded(cells, sides, width):
    for axis, dim in sides:
        count = lax.axis_size(axis)
        head = lax.slice_in_dim(cells, 0, width, axis=dim)
        tail = lax.slice_in_dim(cells, cells.shape[dim] - width, cells.shape[dim], axis=dim)
        cells = jnp.concatenate(
            [
                lax.ppermute(tail, axis, [(i, (i + 1) % count) for i in range(count)]),
                cells,
                lax.ppermute(head, axis, [((i + 1) % count, i) for i in range(count)]),
            ],
            axis=dim,
        )
    return cells


def passed_along(block, axis, distance):
    devices = range(lax.axis_size(axis))
    route = [((i - distance) % len(devices), i) for i in devices]
    return lax.ppermute(block, axis, route)


def normalize(values):
    return values * lax.rsqrt(jnp.mean(values * values, axis=-1, keepdims=True) + EPSILON)


def distance_kernel(offset):
    return jnp.sqrt(offset * offset + SOFTNESS) - SOFT_ROOT


def kernel_slope(offset):
    return offset / jnp.sqrt(offset * offset + SOFTNESS)


def paired():
    return lax.axis_size("member") == 2 and lax.axis_size("grp") == 2


def swapped(block, axis):
    return lax.ppermute(block, axis, [(0, 1), (1, 0)])


def core_swapped(block):
    return lax.ppermute(block, "tile", [(i, i ^ 1) for i in range(lax.axis_size("tile"))])


def shifted(block, distance):
    count = lax.axis_size("tile")
    chips = count // 2
    route = [(i, (i // 2 + distance) % chips * 2 + i % 2) for i in range(count)]
    return lax.ppermute(block, "tile", route)


def tile_sum(values):
    count = lax.axis_size("tile")
    if count & (count - 1):
        return lax.psum(values, "tile")
    step = 1
    while step < count:
        values = values + lax.ppermute(values, "tile", [(i, i ^ step) for i in range(count)])
        step *= 2
    return values


def pick(block, index, dim):
    return lax.dynamic_index_in_dim(block, index, dim, keepdims=False)


def half(block, index, dim):
    size = block.shape[dim] // 2
    return lax.dynamic_slice_in_dim(block, index * size, size, axis=dim)


def halved(block, index, dim, axis):
    got = swapped(half(block, 1 - index, dim).astype(jnp.bfloat16), axis)
    return half(block, index, dim) + got.astype(jnp.float32)


def blend_matrix(local_index, nodes_dev):
    column = jnp.arange(nodes_dev + 2 * HALO, dtype=jnp.int32)[None, :]
    row = jnp.arange(nodes_dev, dtype=jnp.int32)[:, None]
    total = (column == row + HALO).astype(jnp.float32)
    for k in range(NEIGH):
        total = total + jnp.where(column == local_index[:, k : k + 1], 1.0 / NEIGH, 0.0)
    return total.astype(jnp.bfloat16)


def blend_local(normed, matrix):
    extended = padded(normed, (("tile", 0),), HALO)
    return jnp.dot(matrix, extended, preferred_element_type=jnp.float32).astype(jnp.bfloat16)


def unblend_local(grad_blend, matrix):
    nodes_dev = grad_blend.shape[0]
    coarse = lax.reduce_precision(grad_blend, 8, 7)
    fine = (grad_blend - coarse).astype(jnp.bfloat16)
    extended = jnp.dot(
        matrix.T, coarse.astype(jnp.bfloat16), preferred_element_type=jnp.float32
    ) + jnp.dot(matrix.T, fine, preferred_element_type=jnp.float32)
    from_next = passed_along(extended[:HALO], "tile", -1)
    from_prev = passed_along(extended[nodes_dev + HALO :], "tile", 1)
    result = extended[HALO : nodes_dev + HALO]
    result = result.at[nodes_dev - HALO :].add(from_next)
    return result.at[:HALO].add(from_prev)


def core_reduced(left, right):
    count = lax.axis_size("tile")
    core = lax.axis_index("tile") % 2
    grouped = left.reshape(left.shape[0], count // 2, 2, -1)
    rows = left.shape[1] // 2

    def product(which):
        chosen = pick(grouped, which, 2).reshape(left.shape[0], rows)
        return jnp.dot(chosen.T, right, preferred_element_type=jnp.float32)

    got = core_swapped(product(1 - core).astype(jnp.bfloat16))
    total = product(core) + got.astype(jnp.float32)
    return total.reshape(count // 2, -1, right.shape[1])


def reduced_widely(down, up):
    chips = lax.axis_size("tile") // 2
    chip = lax.axis_index("tile") // 2
    totals = []
    for parts in (down, up):
        total = pick(parts, chip, 0)
        for k in range(1, chips):
            sent = pick(parts, (chip + k) % chips, 0).astype(jnp.bfloat16)
            total = total + shifted(sent, k).astype(jnp.float32)
        totals.append(lax.psum(total, ("member", "grp")))
    return tuple(totals)


def reduced(down, up):
    if not paired():
        return reduced_widely(down, up)
    chips = lax.axis_size("tile") // 2
    chip = lax.axis_index("tile") // 2
    x = lax.axis_index("member")
    y = lax.axis_index("grp")
    rows = down.shape[1] // 2
    width = down.shape[2]
    first = jnp.stack([down[:, :rows], up[:, :, :width]])
    second = jnp.stack([down[:, rows:], up[:, :, width:]])
    first = halved(first, x, 2, "member")
    second = halved(second, y, 2, "grp")
    first = halved(first, y, 3, "grp")
    second = halved(second, x, 3, "member")
    both = jnp.stack([first, second])
    total = pick(both, chip, 2)
    for k in range(1, chips):
        sent = pick(both, (chip + k) % chips, 2).astype(jnp.bfloat16)
        total = total + shifted(sent, k).astype(jnp.float32)
    own = total.astype(SHARE)
    grid = [(m, g) for m in range(2) for g in range(2)]

    def from_corner(dm, dg):
        if not (dm or dg):
            return own
        route = [(2 * m + g, 2 * (m ^ dm) + (g ^ dg)) for m, g in grid]
        return lax.ppermute(own, ("member", "grp"), route)

    corners = [from_corner(m, g) for m, g in grid]
    west = [jnp.where(x == 0, corners[g], corners[2 + g]) for g in range(2)]
    east = [jnp.where(x == 0, corners[2 + g], corners[g]) for g in range(2)]

    def ordered(pair):
        return (jnp.where(y == 0, pair[0], pair[1]), jnp.where(y == 0, pair[1], pair[0]))

    (a00, a01), (a10, a11) = ordered(west), ordered(east)

    def tiled(p, q, r, s, part):
        top = jnp.concatenate([p[part], q[part]], axis=2)
        low = jnp.concatenate([r[part], s[part]], axis=2)
        return jnp.concatenate([top, low], axis=1).astype(jnp.float32)

    first = tiled(a00, a01, a10, a11, 0)
    second = tiled(a00, a10, a01, a11, 1)
    return (
        jnp.concatenate([first[0], second[0]], axis=0),
        jnp.concatenate([first[1], second[1]], axis=1),
    )


def reduced_out(left, right):
    chips = lax.axis_size("tile") // 2
    chip = lax.axis_index("tile") // 2
    core = lax.axis_index("tile") % 2
    whole = jnp.dot(left.T, right, preferred_element_type=jnp.float32)
    whole = whole.reshape(chips, 2, -1, right.shape[1])
    total = pick(whole, core, 1) + core_swapped(pick(whole, 1 - core, 1))
    mine = pick(total, chip, 0)
    for k in range(1, chips):
        mine = mine + shifted(pick(total, (chip + k) % chips, 0), k)
    if not paired():
        return lax.psum(mine, ("member", "grp"))
    mine = mine + swapped(mine, "member")
    return mine + swapped(mine, "grp")


def gathered(block, dim):
    if not paired():
        return lax.all_gather(block, "tile", axis=0, tiled=True)
    chips = lax.axis_size("tile") // 2
    chip = lax.axis_index("tile") // 2
    core = lax.axis_index("tile") % 2
    x = lax.axis_index("member")
    y = lax.axis_index("grp")
    first, second = half(block, 0, dim), half(block, 1, dim)
    mine = jnp.stack([half(first, x, dim), half(second, y, dim)])
    columns = jnp.stack([mine] + [shifted(mine, k) for k in range(1, chips)], axis=1)

    def joined(kept, axis, index):
        got = swapped(kept, axis)
        low = jnp.where(index == 0, kept, got)
        high = jnp.where(index == 0, got, kept)
        return [low, high]

    chip_rows = jnp.concatenate(
        joined(columns[0], "member", x) + joined(columns[1], "grp", y), axis=dim + 1
    )
    other = core_swapped(chip_rows)
    order = [(chip - z) % chips for z in range(chips)]
    pieces = []
    for z in range(chips):
        here, there = pick(chip_rows, order[z], 0), pick(other, order[z], 0)
        pieces.append(jnp.where(core == 0, here, there))
        pieces.append(jnp.where(core == 0, there, here))
    return jnp.concatenate(pieces, axis=0)


def gathered_out(block):
    chips = lax.axis_size("tile") // 2
    chip = lax.axis_index("tile") // 2
    core = lax.axis_index("tile") % 2
    other = core_swapped(block)
    pair = jnp.concatenate(
        [jnp.where(core == 0, block, other), jnp.where(core == 0, other, block)], axis=0
    )
    parts = jnp.stack([pair] + [shifted(pair, k) for k in range(1, chips)])
    order = (chip - jnp.arange(chips)) % chips
    return jnp.concatenate([pick(parts, order[z], 0) for z in range(chips)], axis=0)


def shards(latent, noise, area, target, truth, neighbours, w_up, w_down, w_out):
    nodes_dev = latent.shape[0]
    total_nodes = nodes_dev * lax.axis_size("tile")
    row_ids = jnp.arange(nodes_dev, dtype=jnp.int32)
    global_rows = lax.axis_index("tile") * nodes_dev + row_ids
    local_index = (neighbours - global_rows[:, None] + HALO) % total_nodes + row_ids[:, None]
    full_up = [gathered(w_up[l], 1) for l in range(LAYERS)]
    full_down = [gathered(w_down[l], 0) for l in range(LAYERS)]
    full_out = gathered_out(w_out)
    matrix = blend_matrix(local_index, nodes_dev)
    hidden_state = latent.astype(jnp.float32) + noise[0].astype(jnp.float32)
    stored = []
    for layer_index in range(LAYERS):
        blended = blend_local(normalize(hidden_state).astype(jnp.bfloat16), matrix)
        preact = jnp.dot(blended, full_up[layer_index], preferred_element_type=jnp.float32)
        hidden = jax.nn.gelu(preact).astype(jnp.bfloat16)
        stored.append((hidden_state, blended, preact, hidden))
        hidden_state = hidden_state + jnp.dot(
            hidden, full_down[layer_index], preferred_element_type=jnp.float32
        )
    final_state = hidden_state
    final_normed = normalize(final_state).astype(jnp.bfloat16)
    predicted = jnp.dot(final_normed, full_out, preferred_element_type=jnp.float32)
    channels = predicted.shape[1]
    block_size = channels // lax.axis_size(("member", "grp"))
    first_channel = lax.axis_index(("member", "grp")) * block_size
    is_temp = first_channel + jnp.arange(block_size, dtype=jnp.int32) < TEMP
    local_sums = jnp.concatenate(
        [
            jnp.dot(area, predicted[:, :TEMP], precision=lax.Precision.HIGHEST),
            jnp.sum(area)[None],
        ]
    )
    sums = tile_sum(local_sums)
    weighted, area_total = sums[:TEMP], sums[TEMP]
    nudged = predicted.at[:, :TEMP].add(target - weighted / area_total)
    ensemble = lax.all_to_all(
        nudged.T[None], ("member", "grp"), split_axis=1, concat_axis=0, tiled=True
    )
    members = ensemble.shape[0]
    against = ensemble - truth[None]
    skill_term = jnp.mean(distance_kernel(against), axis=0)
    pair_gaps = ensemble[:, None] - ensemble[None, :]
    spread = jnp.sum(distance_kernel(pair_gaps), axis=(0, 1))
    slope_sum = jnp.sum(kernel_slope(pair_gaps), axis=1)
    score_field = skill_term - spread / (2 * members * (members - 1))
    cotangent = kernel_slope(against) / members - slope_sum / (members * (members - 1))
    column_sums = tile_sum(jnp.sum(cotangent, axis=2))
    correction = jnp.where(is_temp[None, :], column_sums, 0.0)
    cotangent = cotangent - area[None, None, :] * (correction[:, :, None] / area_total)
    returned = lax.all_to_all(
        cotangent, ("member", "grp"), split_axis=0, concat_axis=1, tiled=True
    )[0]
    upstream = returned.T.astype(jnp.bfloat16)
    sum_out = reduced_out(final_normed, upstream)
    grad_final = jnp.dot(upstream, full_out.T, preferred_element_type=jnp.float32)
    grad_state = jax.vjp(normalize, final_state)[1](grad_final)[0]
    ups_list = []
    downs_list = []
    for layer_index in reversed(range(LAYERS)):
        hidden_state, blended, preact, hidden = stored[layer_index]
        flowing = grad_state.astype(jnp.bfloat16)
        down = core_reduced(hidden, flowing)
        grad_hidden = jnp.dot(flowing, full_down[layer_index].T, preferred_element_type=jnp.float32)
        grad_preact = jax.vjp(jax.nn.gelu, preact)[1](grad_hidden)[0].astype(jnp.bfloat16)
        sum_down, sum_up = reduced(down, core_reduced(blended, grad_preact))
        downs_list.insert(0, sum_down)
        ups_list.insert(0, sum_up)
        if layer_index == 0:
            break
        grad_blend = jnp.dot(
            grad_preact, full_up[layer_index].T, preferred_element_type=jnp.float32
        )
        grad_normed = unblend_local(grad_blend, matrix)
        grad_state = grad_state + jax.vjp(normalize, hidden_state)[1](grad_normed)[0]
    return (score_field, jnp.stack(ups_list), jnp.stack(downs_list), sum_out)


def solution(mesh):
    return jax.shard_map(
        shards,
        mesh=mesh,
        in_specs=(
            P("tile", None),
            P(("member", "grp"), "tile", None),
            P("tile"),
            P(),
            P(("member", "grp"), "tile"),
            P("tile", None),
            P(None, "tile", None),
            P(None, "tile", None),
            P("tile", None),
        ),
        out_specs=(
            P(("member", "grp"), "tile"),
            P(None, "tile", None),
            P(None, "tile", None),
            P("tile", None),
        ),
        check_vma=False,
    )
```

```python
import jax
import jax.numpy as jnp
from jax import lax
from jax.sharding import PartitionSpec as P

TEMP = 13
NEIGH = 4
HALO = 32
LAYERS = 2


EPSILON = 1e-06
SOFTNESS = 0.25
SOFT_ROOT = 0.5
SHARE = jnp.bfloat16


def padded(cells, sides, width):
    for axis, dim in sides:
        count = lax.axis_size(axis)
        head = lax.slice_in_dim(cells, 0, width, axis=dim)
        tail = lax.slice_in_dim(cells, cells.shape[dim] - width, cells.shape[dim], axis=dim)
        cells = jnp.concatenate(
            [
                lax.ppermute(tail, axis, [(i, (i + 1) % count) for i in range(count)]),
                cells,
                lax.ppermute(head, axis, [((i + 1) % count, i) for i in range(count)]),
            ],
            axis=dim,
        )
    return cells


def passed_along(block, axis, distance):
    devices = range(lax.axis_size(axis))
    route = [((i - distance) % len(devices), i) for i in devices]
    return lax.ppermute(block, axis, route)


def normalize(values):
    return values * lax.rsqrt(jnp.mean(values * values, axis=-1, keepdims=True) + EPSILON)


def distance_kernel(offset):
    return jnp.sqrt(offset * offset + SOFTNESS) - SOFT_ROOT


def kernel_slope(offset):
    return offset / jnp.sqrt(offset * offset + SOFTNESS)


def paired():
    return lax.axis_size("member") == 2 and lax.axis_size("grp") == 2


def swapped(block, axis):
    return lax.ppermute(block, axis, [(0, 1), (1, 0)])


def core_swapped(block):
    return lax.ppermute(block, "tile", [(i, i ^ 1) for i in range(lax.axis_size("tile"))])


def shifted(block, distance):
    count = lax.axis_size("tile")
    chips = count // 2
    route = [(i, (i // 2 + distance) % chips * 2 + i % 2) for i in range(count)]
    return lax.ppermute(block, "tile", route)


def tile_sum(values):
    count = lax.axis_size("tile")
    if count & (count - 1):
        return lax.psum(values, "tile")
    step = 1
    while step < count:
        values = values + lax.ppermute(values, "tile", [(i, i ^ step) for i in range(count)])
        step *= 2
    return values


def pick(block, index, dim):
    return lax.dynamic_index_in_dim(block, index, dim, keepdims=False)


def half(block, index, dim):
    size = block.shape[dim] // 2
    return lax.dynamic_slice_in_dim(block, index * size, size, axis=dim)


def halved(block, index, dim, axis):
    got = swapped(half(block, 1 - index, dim).astype(jnp.bfloat16), axis)
    return half(block, index, dim) + got.astype(jnp.float32)


def blend_matrix(local_index, nodes_dev):
    column = jnp.arange(nodes_dev + 2 * HALO, dtype=jnp.int32)[None, :]
    row = jnp.arange(nodes_dev, dtype=jnp.int32)[:, None]
    total = (column == row + HALO).astype(jnp.float32)
    for k in range(NEIGH):
        total = total + jnp.where(column == local_index[:, k : k + 1], 1.0 / NEIGH, 0.0)
    return total.astype(jnp.bfloat16)


def blend_local(normed, matrix):
    extended = padded(normed, (("tile", 0),), HALO)
    return jnp.dot(matrix, extended, preferred_element_type=jnp.float32).astype(jnp.bfloat16)


def unblend_local(grad_blend, matrix):
    nodes_dev = grad_blend.shape[0]
    coarse = lax.reduce_precision(grad_blend, 8, 7)
    fine = (grad_blend - coarse).astype(jnp.bfloat16)
    extended = jnp.dot(
        matrix.T, coarse.astype(jnp.bfloat16), preferred_element_type=jnp.float32
    ) + jnp.dot(matrix.T, fine, preferred_element_type=jnp.float32)
    from_next = passed_along(extended[:HALO], "tile", -1)
    from_prev = passed_along(extended[nodes_dev + HALO :], "tile", 1)
    result = extended[HALO : nodes_dev + HALO]
    result = result.at[nodes_dev - HALO :].add(from_next)
    return result.at[:HALO].add(from_prev)


def core_reduced(left, right):
    count = lax.axis_size("tile")
    core = lax.axis_index("tile") % 2
    grouped = left.reshape(left.shape[0], count // 2, 2, -1)
    rows = left.shape[1] // 2

    def product(which):
        chosen = pick(grouped, which, 2).reshape(left.shape[0], rows)
        return jnp.dot(chosen.T, right, preferred_element_type=jnp.float32)

    got = core_swapped(product(1 - core).astype(jnp.bfloat16))
    total = product(core) + got.astype(jnp.float32)
    return total.reshape(count // 2, -1, right.shape[1])


def reduced_widely(down, up):
    chips = lax.axis_size("tile") // 2
    chip = lax.axis_index("tile") // 2
    totals = []
    for parts in (down, up):
        total = pick(parts, chip, 0)
        for k in range(1, chips):
            sent = pick(parts, (chip + k) % chips, 0).astype(jnp.bfloat16)
            total = total + shifted(sent, k).astype(jnp.float32)
        totals.append(lax.psum(total, ("member", "grp")))
    return tuple(totals)


def reduced(down, up):
    if not paired():
        return reduced_widely(down, up)
    chips = lax.axis_size("tile") // 2
    chip = lax.axis_index("tile") // 2
    x = lax.axis_index("member")
    y = lax.axis_index("grp")
    rows = down.shape[1] // 2
    width = down.shape[2]
    first = jnp.stack([down[:, :rows], up[:, :, :width]])
    second = jnp.stack([down[:, rows:], up[:, :, width:]])
    first = halved(first, x, 2, "member")
    second = halved(second, y, 2, "grp")
    first = halved(first, y, 3, "grp")
    second = halved(second, x, 3, "member")
    both = jnp.stack([first, second])
    total = pick(both, chip, 2)
    for k in range(1, chips):
        sent = pick(both, (chip + k) % chips, 2).astype(jnp.bfloat16)
        total = total + shifted(sent, k).astype(jnp.float32)
    own = total.astype(SHARE)
    grid = [(m, g) for m in range(2) for g in range(2)]

    def from_corner(dm, dg):
        if not (dm or dg):
            return own
        route = [(2 * m + g, 2 * (m ^ dm) + (g ^ dg)) for m, g in grid]
        return lax.ppermute(own, ("member", "grp"), route)

    corners = [from_corner(m, g) for m, g in grid]
    west = [jnp.where(x == 0, corners[g], corners[2 + g]) for g in range(2)]
    east = [jnp.where(x == 0, corners[2 + g], corners[g]) for g in range(2)]

    def ordered(pair):
        return (jnp.where(y == 0, pair[0], pair[1]), jnp.where(y == 0, pair[1], pair[0]))

    (a00, a01), (a10, a11) = ordered(west), ordered(east)

    def tiled(p, q, r, s, part):
        top = jnp.concatenate([p[part], q[part]], axis=2)
        low = jnp.concatenate([r[part], s[part]], axis=2)
        return jnp.concatenate([top, low], axis=1).astype(jnp.float32)

    first = tiled(a00, a01, a10, a11, 0)
    second = tiled(a00, a10, a01, a11, 1)
    return (
        jnp.concatenate([first[0], second[0]], axis=0),
        jnp.concatenate([first[1], second[1]], axis=1),
    )


def reduced_out(left, right):
    chips = lax.axis_size("tile") // 2
    chip = lax.axis_index("tile") // 2
    core = lax.axis_index("tile") % 2
    whole = jnp.dot(left.T, right, preferred_element_type=jnp.float32)
    whole = whole.reshape(chips, 2, -1, right.shape[1])
    total = pick(whole, core, 1) + core_swapped(pick(whole, 1 - core, 1))
    mine = pick(total, chip, 0)
    for k in range(1, chips):
        mine = mine + shifted(pick(total, (chip + k) % chips, 0), k)
    if not paired():
        return lax.psum(mine, ("member", "grp"))
    mine = mine + swapped(mine, "member")
    return mine + swapped(mine, "grp")


def fetched(down, up):
    chips = lax.axis_size("tile") // 2
    rows, width = down.shape[0] // 4, down.shape[1]
    lower = down.reshape(2, 2, rows, width)
    upper = jnp.stack([up[:, :width], up[:, width:]]).reshape(2, 2, rows, width)
    first = jnp.stack([lower[0], upper[0]])
    second = jnp.stack([lower[1], upper[1]])
    mine = jnp.stack(
        [
            pick(first, lax.axis_index("member"), 1),
            pick(second, lax.axis_index("grp"), 1),
        ]
    )
    return [mine] + [shifted(mine, k) for k in range(1, chips)]


def spread(columns):
    chips = len(columns)
    chip = lax.axis_index("tile") // 2
    core = lax.axis_index("tile") % 2
    kept = jnp.stack(columns, axis=1)
    halves = []
    for part, axis in enumerate(("member", "grp")):
        got = swapped(kept[part], axis)
        index = lax.axis_index(axis)
        low = jnp.where(index == 0, kept[part], got)
        high = jnp.where(index == 0, got, kept[part])
        halves.append(jnp.stack([low, high], axis=2))
    whole = jnp.stack(halves, axis=1)
    other = core_swapped(whole)
    downs, ups = [], []
    for z in range(chips):
        here = pick(whole, (chip - z) % chips, 0)
        there = pick(other, (chip - z) % chips, 0)
        for block in (
            jnp.where(core == 0, here, there),
            jnp.where(core == 0, there, here),
        ):
            width = block.shape[-1]
            downs.append(block[:, 0].reshape(-1, width))
            sides = block[:, 1].reshape(2, -1, width)
            ups.append(jnp.concatenate([sides[0], sides[1]], axis=1))
    return jnp.concatenate(downs, axis=0), jnp.concatenate(ups, axis=0)


def gathered_weights(w_up, w_down, w_out):
    if not paired():
        ups = [lax.all_gather(w_up[l], "tile", axis=0, tiled=True) for l in range(LAYERS)]
        downs = [lax.all_gather(w_down[l], "tile", axis=0, tiled=True) for l in range(LAYERS)]
        return ups, downs, gathered_out(w_out)
    ups, downs = [], []
    for l in range(LAYERS):
        columns = fetched(w_down[l], w_up[l])
        columns, w_up, w_down, w_out = lax.optimization_barrier((columns, w_up, w_down, w_out))
        down, up = spread(columns)
        downs.append(down)
        ups.append(up)
    return ups, downs, gathered_out(w_out)


def gathered_out(block):
    chips = lax.axis_size("tile") // 2
    chip = lax.axis_index("tile") // 2
    core = lax.axis_index("tile") % 2
    other = core_swapped(block)
    pair = jnp.concatenate(
        [jnp.where(core == 0, block, other), jnp.where(core == 0, other, block)], axis=0
    )
    parts = jnp.stack([pair] + [shifted(pair, k) for k in range(1, chips)])
    order = (chip - jnp.arange(chips)) % chips
    return jnp.concatenate([pick(parts, order[z], 0) for z in range(chips)], axis=0)


def shards(latent, noise, area, target, truth, neighbours, w_up, w_down, w_out):
    nodes_dev = latent.shape[0]
    total_nodes = nodes_dev * lax.axis_size("tile")
    row_ids = jnp.arange(nodes_dev, dtype=jnp.int32)
    global_rows = lax.axis_index("tile") * nodes_dev + row_ids
    local_index = (neighbours - global_rows[:, None] + HALO) % total_nodes + row_ids[:, None]
    full_up, full_down, full_out = gathered_weights(w_up, w_down, w_out)
    matrix = blend_matrix(local_index, nodes_dev)
    hidden_state = latent.astype(jnp.float32) + noise[0].astype(jnp.float32)
    stored = []
    for layer_index in range(LAYERS):
        blended = blend_local(normalize(hidden_state).astype(jnp.bfloat16), matrix)
        preact = jnp.dot(blended, full_up[layer_index], preferred_element_type=jnp.float32)
        hidden = jax.nn.gelu(preact).astype(jnp.bfloat16)
        stored.append((hidden_state, blended, preact, hidden))
        hidden_state = hidden_state + jnp.dot(
            hidden, full_down[layer_index], preferred_element_type=jnp.float32
        )
    final_state = hidden_state
    final_normed = normalize(final_state).astype(jnp.bfloat16)
    predicted = jnp.dot(final_normed, full_out, preferred_element_type=jnp.float32)
    channels = predicted.shape[1]
    block_size = channels // lax.axis_size(("member", "grp"))
    first_channel = lax.axis_index(("member", "grp")) * block_size
    is_temp = first_channel + jnp.arange(block_size, dtype=jnp.int32) < TEMP
    local_sums = jnp.concatenate(
        [
            jnp.dot(area, predicted[:, :TEMP], precision=lax.Precision.HIGHEST),
            jnp.sum(area)[None],
        ]
    )
    sums = tile_sum(local_sums)
    weighted, area_total = sums[:TEMP], sums[TEMP]
    nudged = predicted.at[:, :TEMP].add(target - weighted / area_total)
    ensemble = lax.all_to_all(
        nudged.T[None], ("member", "grp"), split_axis=1, concat_axis=0, tiled=True
    )
    members = ensemble.shape[0]
    against = ensemble - truth[None]
    skill_term = jnp.mean(distance_kernel(against), axis=0)
    pair_gaps = ensemble[:, None] - ensemble[None, :]
    spread = jnp.sum(distance_kernel(pair_gaps), axis=(0, 1))
    slope_sum = jnp.sum(kernel_slope(pair_gaps), axis=1)
    score_field = skill_term - spread / (2 * members * (members - 1))
    cotangent = kernel_slope(against) / members - slope_sum / (members * (members - 1))
    column_sums = tile_sum(jnp.sum(cotangent, axis=2))
    correction = jnp.where(is_temp[None, :], column_sums, 0.0)
    cotangent = cotangent - area[None, None, :] * (correction[:, :, None] / area_total)
    returned = lax.all_to_all(
        cotangent, ("member", "grp"), split_axis=0, concat_axis=1, tiled=True
    )[0]
    upstream = returned.T.astype(jnp.bfloat16)
    sum_out = reduced_out(final_normed, upstream)
    grad_final = jnp.dot(upstream, full_out.T, preferred_element_type=jnp.float32)
    grad_state = jax.vjp(normalize, final_state)[1](grad_final)[0]
    ups_list = []
    downs_list = []
    for layer_index in reversed(range(LAYERS)):
        hidden_state, blended, preact, hidden = stored[layer_index]
        flowing = grad_state.astype(jnp.bfloat16)
        down = core_reduced(hidden, flowing)
        grad_hidden = jnp.dot(flowing, full_down[layer_index].T, preferred_element_type=jnp.float32)
        grad_preact = jax.vjp(jax.nn.gelu, preact)[1](grad_hidden)[0].astype(jnp.bfloat16)
        sum_down, sum_up = reduced(down, core_reduced(blended, grad_preact))
        downs_list.insert(0, sum_down)
        ups_list.insert(0, sum_up)
        if layer_index == 0:
            break
        grad_blend = jnp.dot(
            grad_preact, full_up[layer_index].T, preferred_element_type=jnp.float32
        )
        grad_normed = unblend_local(grad_blend, matrix)
        grad_state = grad_state + jax.vjp(normalize, hidden_state)[1](grad_normed)[0]
    return (score_field, jnp.stack(ups_list), jnp.stack(downs_list), sum_out)


def solution(mesh):
    return jax.shard_map(
        shards,
        mesh=mesh,
        in_specs=(
            P("tile", None),
            P(("member", "grp"), "tile", None),
            P("tile"),
            P(),
            P(("member", "grp"), "tile"),
            P("tile", None),
            P(None, "tile", None),
            P(None, "tile", None),
            P("tile", None),
        ),
        out_specs=(
            P(("member", "grp"), "tile"),
            P(None, "tile", None),
            P(None, "tile", None),
            P("tile", None),
        ),
        check_vma=False,
    )
```

```python
import jax
import jax.numpy as jnp
from jax import lax
from jax.sharding import PartitionSpec as P

TEMP = 13
NEIGH = 4
HALO = 32
LAYERS = 2


EPSILON = 1e-06
SOFTNESS = 0.25
SOFT_ROOT = 0.5
SHARE = jnp.bfloat16


def padded(cells, sides, width):
    for axis, dim in sides:
        count = lax.axis_size(axis)
        head = lax.slice_in_dim(cells, 0, width, axis=dim)
        tail = lax.slice_in_dim(cells, cells.shape[dim] - width, cells.shape[dim], axis=dim)
        cells = jnp.concatenate(
            [
                lax.ppermute(tail, axis, [(i, (i + 1) % count) for i in range(count)]),
                cells,
                lax.ppermute(head, axis, [((i + 1) % count, i) for i in range(count)]),
            ],
            axis=dim,
        )
    return cells


def passed_along(block, axis, distance):
    devices = range(lax.axis_size(axis))
    route = [((i - distance) % len(devices), i) for i in devices]
    return lax.ppermute(block, axis, route)


def normalize(values):
    return values * lax.rsqrt(jnp.mean(values * values, axis=-1, keepdims=True) + EPSILON)


def distance_kernel(offset):
    return jnp.sqrt(offset * offset + SOFTNESS) - SOFT_ROOT


def kernel_slope(offset):
    return offset / jnp.sqrt(offset * offset + SOFTNESS)


def paired():
    return lax.axis_size("member") == 2 and lax.axis_size("grp") == 2


def swapped(block, axis):
    return lax.ppermute(block, axis, [(0, 1), (1, 0)])


def core_swapped(block):
    return lax.ppermute(block, "tile", [(i, i ^ 1) for i in range(lax.axis_size("tile"))])


def shifted(block, distance):
    count = lax.axis_size("tile")
    chips = count // 2
    route = [(i, (i // 2 + distance) % chips * 2 + i % 2) for i in range(count)]
    return lax.ppermute(block, "tile", route)


def tile_sum(values):
    count = lax.axis_size("tile")
    if count & (count - 1):
        return lax.psum(values, "tile")
    step = 1
    while step < count:
        values = values + lax.ppermute(values, "tile", [(i, i ^ step) for i in range(count)])
        step *= 2
    return values


def pick(block, index, dim):
    return lax.dynamic_index_in_dim(block, index, dim, keepdims=False)


def half(block, index, dim):
    size = block.shape[dim] // 2
    return lax.dynamic_slice_in_dim(block, index * size, size, axis=dim)


def halved(block, index, dim, axis):
    got = swapped(half(block, 1 - index, dim).astype(jnp.bfloat16), axis)
    return half(block, index, dim) + got.astype(jnp.float32)


def blend_matrix(local_index, nodes_dev):
    column = jnp.arange(nodes_dev + 2 * HALO, dtype=jnp.int32)[None, :]
    row = jnp.arange(nodes_dev, dtype=jnp.int32)[:, None]
    total = (column == row + HALO).astype(jnp.float32)
    for k in range(NEIGH):
        total = total + jnp.where(column == local_index[:, k : k + 1], 1.0 / NEIGH, 0.0)
    return total.astype(jnp.bfloat16)


def blend_local(normed, matrix):
    extended = padded(normed, (("tile", 0),), HALO)
    return jnp.dot(matrix, extended, preferred_element_type=jnp.float32).astype(jnp.bfloat16)


def unblend_local(grad_blend, matrix):
    nodes_dev = grad_blend.shape[0]
    coarse = lax.reduce_precision(grad_blend, 8, 7)
    fine = (grad_blend - coarse).astype(jnp.bfloat16)
    extended = jnp.dot(
        matrix.T, coarse.astype(jnp.bfloat16), preferred_element_type=jnp.float32
    ) + jnp.dot(matrix.T, fine, preferred_element_type=jnp.float32)
    from_next = passed_along(extended[:HALO], "tile", -1)
    from_prev = passed_along(extended[nodes_dev + HALO :], "tile", 1)
    result = extended[HALO : nodes_dev + HALO]
    result = result.at[nodes_dev - HALO :].add(from_next)
    return result.at[:HALO].add(from_prev)


def core_reduced(left, right):
    count = lax.axis_size("tile")
    core = lax.axis_index("tile") % 2
    grouped = left.reshape(left.shape[0], count // 2, 2, -1)
    rows = left.shape[1] // 2

    def product(which):
        chosen = pick(grouped, which, 2).reshape(left.shape[0], rows)
        return jnp.dot(chosen.T, right, preferred_element_type=jnp.float32)

    got = core_swapped(product(1 - core).astype(jnp.bfloat16))
    total = product(core) + got.astype(jnp.float32)
    return total.reshape(count // 2, -1, right.shape[1])


def reduced_widely(down, up):
    chips = lax.axis_size("tile") // 2
    chip = lax.axis_index("tile") // 2
    totals = []
    for parts in (down, up):
        total = pick(parts, chip, 0)
        for k in range(1, chips):
            sent = pick(parts, (chip + k) % chips, 0).astype(jnp.bfloat16)
            total = total + shifted(sent, k).astype(jnp.float32)
        totals.append(lax.psum(total, ("member", "grp")))
    return tuple(totals)


def reduction_begun(down, up):
    if not paired():
        return down, up
    rows = down.shape[1] // 2
    width = down.shape[2]
    first = jnp.stack([down[:, :rows], up[:, :, :width]])
    second = jnp.stack([down[:, rows:], up[:, :, width:]])
    return (
        halved(first, lax.axis_index("member"), 2, "member"),
        halved(second, lax.axis_index("grp"), 2, "grp"),
    )


def reduced(first, second):
    if not paired():
        return reduced_widely(first, second)
    chips = lax.axis_size("tile") // 2
    chip = lax.axis_index("tile") // 2
    x = lax.axis_index("member")
    y = lax.axis_index("grp")
    first = halved(first, y, 3, "grp")
    second = halved(second, x, 3, "member")
    both = jnp.stack([first, second])
    total = pick(both, chip, 2)
    for k in range(1, chips):
        sent = pick(both, (chip + k) % chips, 2).astype(jnp.bfloat16)
        total = total + shifted(sent, k).astype(jnp.float32)
    own = total.astype(SHARE)
    grid = [(m, g) for m in range(2) for g in range(2)]

    def from_corner(dm, dg):
        if not (dm or dg):
            return own
        route = [(2 * m + g, 2 * (m ^ dm) + (g ^ dg)) for m, g in grid]
        return lax.ppermute(own, ("member", "grp"), route)

    corners = [from_corner(m, g) for m, g in grid]
    west = [jnp.where(x == 0, corners[g], corners[2 + g]) for g in range(2)]
    east = [jnp.where(x == 0, corners[2 + g], corners[g]) for g in range(2)]

    def ordered(pair):
        return (jnp.where(y == 0, pair[0], pair[1]), jnp.where(y == 0, pair[1], pair[0]))

    (a00, a01), (a10, a11) = ordered(west), ordered(east)

    def tiled(p, q, r, s, part):
        top = jnp.concatenate([p[part], q[part]], axis=2)
        low = jnp.concatenate([r[part], s[part]], axis=2)
        return jnp.concatenate([top, low], axis=1).astype(jnp.float32)

    first = tiled(a00, a01, a10, a11, 0)
    second = tiled(a00, a10, a01, a11, 1)
    return (
        jnp.concatenate([first[0], second[0]], axis=0),
        jnp.concatenate([first[1], second[1]], axis=1),
    )


def reduced_out(left, right):
    chips = lax.axis_size("tile") // 2
    chip = lax.axis_index("tile") // 2
    core = lax.axis_index("tile") % 2
    whole = jnp.dot(left.T, right, preferred_element_type=jnp.float32)
    whole = whole.reshape(chips, 2, -1, right.shape[1])
    total = pick(whole, core, 1) + core_swapped(pick(whole, 1 - core, 1))
    mine = pick(total, chip, 0)
    for k in range(1, chips):
        mine = mine + shifted(pick(total, (chip + k) % chips, 0), k)
    if not paired():
        return lax.psum(mine, ("member", "grp"))
    mine = mine + swapped(mine, "member")
    return mine + swapped(mine, "grp")


def fetched(down, up):
    chips = lax.axis_size("tile") // 2
    rows, width = down.shape[0] // 4, down.shape[1]
    lower = down.reshape(2, 2, rows, width)
    upper = jnp.stack([up[:, :width], up[:, width:]]).reshape(2, 2, rows, width)
    first = jnp.stack([lower[0], upper[0]])
    second = jnp.stack([lower[1], upper[1]])
    mine = jnp.stack(
        [
            pick(first, lax.axis_index("member"), 1),
            pick(second, lax.axis_index("grp"), 1),
        ]
    )
    return [mine] + [shifted(mine, k) for k in range(1, chips)]


def spread(columns):
    chips = len(columns)
    chip = lax.axis_index("tile") // 2
    core = lax.axis_index("tile") % 2
    kept = jnp.stack(columns, axis=1)
    halves = []
    for part, axis in enumerate(("member", "grp")):
        got = swapped(kept[part], axis)
        index = lax.axis_index(axis)
        low = jnp.where(index == 0, kept[part], got)
        high = jnp.where(index == 0, got, kept[part])
        halves.append(jnp.stack([low, high], axis=2))
    whole = jnp.stack(halves, axis=1)
    other = core_swapped(whole)
    downs, ups = [], []
    for z in range(chips):
        here = pick(whole, (chip - z) % chips, 0)
        there = pick(other, (chip - z) % chips, 0)
        for block in (
            jnp.where(core == 0, here, there),
            jnp.where(core == 0, there, here),
        ):
            width = block.shape[-1]
            downs.append(block[:, 0].reshape(-1, width))
            sides = block[:, 1].reshape(2, -1, width)
            ups.append(jnp.concatenate([sides[0], sides[1]], axis=1))
    return jnp.concatenate(downs, axis=0), jnp.concatenate(ups, axis=0)


def gathered_weights(w_up, w_down, w_out, early):
    if not paired():
        ups = [lax.all_gather(w_up[l], "tile", axis=0, tiled=True) for l in range(LAYERS)]
        downs = [lax.all_gather(w_down[l], "tile", axis=0, tiled=True) for l in range(LAYERS)]
        return ups, downs, gathered_out(w_out), early
    ups, downs = [], []
    for l in range(LAYERS):
        columns = fetched(w_down[l], w_up[l])
        if l == 0:
            columns, w_up, w_down, w_out, early = lax.optimization_barrier(
                (columns, w_up, w_down, w_out, early)
            )
        down, up = spread(columns)
        downs.append(down)
        ups.append(up)
    return ups, downs, gathered_out(w_out), early


def gathered_out(block):
    chips = lax.axis_size("tile") // 2
    chip = lax.axis_index("tile") // 2
    core = lax.axis_index("tile") % 2
    other = core_swapped(block)
    pair = jnp.concatenate(
        [jnp.where(core == 0, block, other), jnp.where(core == 0, other, block)], axis=0
    )
    parts = jnp.stack([pair] + [shifted(pair, k) for k in range(1, chips)])
    order = (chip - jnp.arange(chips)) % chips
    return jnp.concatenate([pick(parts, order[z], 0) for z in range(chips)], axis=0)


def shards(latent, noise, area, target, truth, neighbours, w_up, w_down, w_out):
    nodes_dev = latent.shape[0]
    total_nodes = nodes_dev * lax.axis_size("tile")
    row_ids = jnp.arange(nodes_dev, dtype=jnp.int32)
    global_rows = lax.axis_index("tile") * nodes_dev + row_ids
    local_index = (neighbours - global_rows[:, None] + HALO) % total_nodes + row_ids[:, None]
    matrix = blend_matrix(local_index, nodes_dev)
    hidden_state = latent.astype(jnp.float32) + noise[0].astype(jnp.float32)
    early = (
        hidden_state,
        blend_local(normalize(hidden_state).astype(jnp.bfloat16), matrix),
        matrix,
    )
    full_up, full_down, full_out, early = gathered_weights(w_up, w_down, w_out, early)
    hidden_state, blended, matrix = early
    stored = []
    for layer_index in range(LAYERS):
        if layer_index:
            blended = blend_local(normalize(hidden_state).astype(jnp.bfloat16), matrix)
        preact = jnp.dot(blended, full_up[layer_index], preferred_element_type=jnp.float32)
        hidden = jax.nn.gelu(preact).astype(jnp.bfloat16)
        stored.append((hidden_state, blended, preact, hidden))
        hidden_state = hidden_state + jnp.dot(
            hidden, full_down[layer_index], preferred_element_type=jnp.float32
        )
    final_state = hidden_state
    final_normed = normalize(final_state).astype(jnp.bfloat16)
    predicted = jnp.dot(final_normed, full_out, preferred_element_type=jnp.float32)
    channels = predicted.shape[1]
    block_size = channels // lax.axis_size(("member", "grp"))
    first_channel = lax.axis_index(("member", "grp")) * block_size
    is_temp = first_channel + jnp.arange(block_size, dtype=jnp.int32) < TEMP
    local_sums = jnp.concatenate(
        [
            jnp.dot(area, predicted[:, :TEMP], precision=lax.Precision.HIGHEST),
            jnp.sum(area)[None],
        ]
    )
    sums = tile_sum(local_sums)
    weighted, area_total = sums[:TEMP], sums[TEMP]
    nudged = predicted.at[:, :TEMP].add(target - weighted / area_total)
    ensemble = lax.all_to_all(
        nudged.T[None], ("member", "grp"), split_axis=1, concat_axis=0, tiled=True
    )
    members = ensemble.shape[0]
    against = ensemble - truth[None]
    skill_term = jnp.mean(distance_kernel(against), axis=0)
    pair_gaps = ensemble[:, None] - ensemble[None, :]
    spread = jnp.sum(distance_kernel(pair_gaps), axis=(0, 1))
    slope_sum = jnp.sum(kernel_slope(pair_gaps), axis=1)
    score_field = skill_term - spread / (2 * members * (members - 1))
    cotangent = kernel_slope(against) / members - slope_sum / (members * (members - 1))
    column_sums = tile_sum(jnp.sum(cotangent, axis=2))
    correction = jnp.where(is_temp[None, :], column_sums, 0.0)
    cotangent = cotangent - area[None, None, :] * (correction[:, :, None] / area_total)
    returned = lax.all_to_all(
        cotangent, ("member", "grp"), split_axis=0, concat_axis=1, tiled=True
    )[0]
    upstream = returned.T.astype(jnp.bfloat16)
    sum_out = reduced_out(final_normed, upstream)
    grad_final = jnp.dot(upstream, full_out.T, preferred_element_type=jnp.float32)
    grad_state = jax.vjp(normalize, final_state)[1](grad_final)[0]
    begun = []
    for layer_index in reversed(range(LAYERS)):
        hidden_state, blended, preact, hidden = stored[layer_index]
        flowing = grad_state.astype(jnp.bfloat16)
        moving = flowing
        if begun:
            begun[-1], moving = lax.optimization_barrier((begun[-1], flowing))
        down = core_reduced(hidden, moving)
        grad_hidden = jnp.dot(flowing, full_down[layer_index].T, preferred_element_type=jnp.float32)
        grad_preact = jax.vjp(jax.nn.gelu, preact)[1](grad_hidden)[0].astype(jnp.bfloat16)
        begun.append(reduction_begun(down, core_reduced(blended, grad_preact)))
        if layer_index == 0:
            break
        grad_blend = jnp.dot(
            grad_preact, full_up[layer_index].T, preferred_element_type=jnp.float32
        )
        grad_normed = unblend_local(grad_blend, matrix)
        grad_state = grad_state + jax.vjp(normalize, hidden_state)[1](grad_normed)[0]
    sums = [reduced(*parts) for parts in reversed(begun)]
    sum_down = jnp.stack([pair[0] for pair in sums])
    sum_up = jnp.stack([pair[1] for pair in sums])
    return (score_field, sum_up, sum_down, sum_out)


def solution(mesh):
    return jax.shard_map(
        shards,
        mesh=mesh,
        in_specs=(
            P("tile", None),
            P(("member", "grp"), "tile", None),
            P("tile"),
            P(),
            P(("member", "grp"), "tile"),
            P("tile", None),
            P(None, "tile", None),
            P(None, "tile", None),
            P("tile", None),
        ),
        out_specs=(
            P(("member", "grp"), "tile"),
            P(None, "tile", None),
            P(None, "tile", None),
            P("tile", None),
        ),
        check_vma=False,
    )
```
